32 devices in a mesh: tm: 8 (over z, x), feat: 4 (over y, core).
Axes of the slice: x: 2, y: 2, z: 4, core: 2. Of those that a mesh axis runs over, the one named last changes fastest.
Arguments:
- activations: bfloat16 [20480, 2048], P(('tm', 'feat')), may hold values from -19 to 19
- targets: bfloat16 [20480, 128], P(('tm', 'feat')), may hold values from -8 to 8
- span_of: int32 [20480], P(('tm', 'feat')), may hold values from 0 to 7, as said below
Outputs:
- predictions: bfloat16 [20480, 128], P(('tm', 'feat'))
- surprise: float32 [20480], P(('tm', 'feat'))
The draws below stay inside these ranges and needn't reach their ends.
Inputs may be any that keep to these rules, and one draw needn't show every extreme that they name: `span_of`: in each aligned block of 640 rows (the rows of one device) every span from 0 to 7 appears exactly 80 times.
All inputs are finite; a program needn't handle non-finite values.
Results may differ from the reference program's by a relative error of at most 0.0049.
Values may be sent and summed in bfloat16 or wider, within the bound.
A program may use at most 320 MiB of HBM per device.

```python
import jax
import jax.numpy as jnp
from jax import lax

D = 2048
K = 128
ITERS = 3
TOK_DEV = 640
SPANS = 8
SPAN_SHARE = 80
SPAN_ROWS = 2560
TOKENS = 20480


def latent_field(key):
    base = jax.random.fold_in(key, 11)
    field = jnp.clip(jax.random.normal(base, (TOKENS, D), jnp.float32), -6.0, 6.0)
    return field


def draw_activations(key, part):
    field = latent_field(key)
    spread = jax.random.uniform(jax.random.fold_in(key, 12), (D,), jnp.float32, -1.15, 1.15)
    return (field * jnp.exp(spread)).astype(jnp.bfloat16)


def draw_targets(key, part):
    field = latent_field(key)
    picks = jax.random.randint(jax.random.fold_in(key, 13), (4, K), 0, D)
    coefs = 0.5 * jnp.clip(jax.random.normal(jax.random.fold_in(key, 14), (4, K), jnp.float32), -3.0, 3.0)
    noise = jnp.clip(jax.random.normal(jax.random.fold_in(key, 15), (TOKENS, K), jnp.float32), -6.0, 6.0)
    total = 0.5 * noise
    for slot in range(4):
        total = total + 0.8 * coefs[slot] * jnp.take(field, picks[slot], axis=1)
    return jnp.clip(total, -8.0, 8.0).astype(jnp.bfloat16)


def draw_span_of(key, part):
    blocks = TOKENS // TOK_DEV
    pattern = (jnp.arange(TOK_DEV, dtype=jnp.int32) // SPAN_SHARE).astype(jnp.int32)
    keys = jax.random.split(jax.random.fold_in(key, 21), blocks)
    mixed = jax.vmap(lambda single: jax.random.permutation(single, pattern))(keys)
    return mixed.reshape(-1).astype(jnp.int32)


def setup_inputs(seed: int = 0) -> dict:
    streams_of = jax.random.split(jax.random.key(seed), 4)
    return {
        "activations": draw_activations(jax.random.fold_in(streams_of[3], 71), 0),
        "targets": draw_targets(jax.random.fold_in(streams_of[3], 71), 0),
        "span_of": draw_span_of(jax.random.fold_in(streams_of[3], 71), 0),
    }


RIDGE = 0.1
TINY = 1e-6


def solve_span(gram_prefix, cross_prefix, seen):
    scale = 1.0 / jnp.maximum(seen, 1.0)
    rhs = scale * cross_prefix
    residual = rhs
    direction = rhs
    norm_now = jnp.sum(residual * residual, axis=0)
    solution = jnp.zeros_like(rhs)
    for step in range(ITERS):
        image = scale * jnp.dot(gram_prefix, direction, precision=lax.Precision.HIGHEST, preferred_element_type=jnp.float32) + RIDGE * direction
        alpha = norm_now / (jnp.sum(direction * image, axis=0) + TINY)
        solution = solution + alpha * direction
        if step + 1 < ITERS:
            residual = residual - alpha * image
            norm_next = jnp.sum(residual * residual, axis=0)
            direction = residual + (norm_next / (norm_now + TINY)) * direction
            norm_now = norm_next
    return solution


def reference(activations, targets, span_of):
    order = jnp.argsort(span_of, stable=True).astype(jnp.int32)
    grouped_x = activations[order].reshape(SPANS, SPAN_ROWS, D)
    grouped_y = targets[order].reshape(SPANS, SPAN_ROWS, K)

    def advance(carry, inputs):
        gram_prefix, cross_prefix = carry
        index, rows_x, rows_y = inputs
        seen = (index * SPAN_ROWS).astype(jnp.float32)
        solution = solve_span(gram_prefix, cross_prefix, seen)
        predicted = jnp.dot(rows_x, solution.astype(jnp.bfloat16), preferred_element_type=jnp.float32).astype(jnp.bfloat16)
        wide_x = rows_x.astype(jnp.float32)
        gram_part = jnp.dot(wide_x.T, wide_x, precision=lax.Precision.HIGHEST, preferred_element_type=jnp.float32)
        cross_part = jnp.dot(wide_x.T, rows_y.astype(jnp.float32), precision=lax.Precision.HIGHEST, preferred_element_type=jnp.float32)
        return (gram_prefix + gram_part, cross_prefix + cross_part), predicted

    start = (jnp.zeros((D, D), jnp.float32), jnp.zeros((D, K), jnp.float32))
    indices = jnp.arange(SPANS, dtype=jnp.int32)
    _, predicted = lax.scan(advance, start, (indices, grouped_x, grouped_y))
    predictions = jnp.zeros((TOKENS, K), jnp.bfloat16).at[order].set(predicted.reshape(TOKENS, K))
    error = targets.astype(jnp.float32) - predictions.astype(jnp.float32)
    surprise = jnp.mean(error * error, axis=1)
    return predictions, surprise
```

```python
import jax
import jax.numpy as jnp
from jax import lax
from jax.sharding import PartitionSpec as P

ITERS = 3
RIDGE = 0.1
TINY = 1e-06
AXES = ("tm", "feat")


def body(activations, targets, span_of):
    spans = lax.axis_size("tm")
    feat_count = lax.axis_size("feat")
    devices = spans * feat_count
    tok_dev, width = activations.shape
    n_targets = targets.shape[1]
    rows = spans * n_targets
    own = rows // devices
    place = lax.axis_index("tm") * feat_count + lax.axis_index("feat")

    span_ids = jnp.arange(spans, dtype=jnp.int32)
    earlier = (span_of[:, None] < span_ids[None, :])[:, :, None]
    here = (span_of[:, None] == span_ids[None, :])[:, :, None]

    def back(masked):
        part = lax.dot_general(
            masked.reshape(tok_dev, rows),
            activations,
            (((0,), (0,)), ((), ())),
            preferred_element_type=jnp.float32,
        )
        return lax.psum_scatter(part, AXES, scatter_dimension=0, tiled=True)

    row_span = (place * own + jnp.arange(own, dtype=jnp.int32)) // n_targets
    seen = (row_span * (tok_dev * feat_count)).astype(jnp.float32)
    scale = (1.0 / jnp.maximum(seen, 1.0))[:, None]

    zero = jnp.zeros((), targets.dtype)
    rhs = scale * back(jnp.where(earlier, targets[:, None, :], zero))
    residual = rhs
    direction = rhs
    norm_now = jnp.sum(rhs * rhs, axis=1, keepdims=True)
    alphas = []
    kept = []
    for step in range(ITERS):
        sent = direction.astype(jnp.bfloat16)
        direction = sent.astype(jnp.float32)
        everywhere = lax.all_gather(sent, AXES, axis=0, tiled=True)
        image_t = lax.dot_general(
            activations,
            everywhere,
            (((1,), (1,)), ((), ())),
            preferred_element_type=jnp.float32,
        ).reshape(tok_dev, spans, n_targets)
        kept.append(jnp.sum(jnp.where(here, image_t, 0.0), axis=1))
        if step + 1 < ITERS:
            masked = jnp.where(earlier, image_t, 0.0).astype(jnp.bfloat16)
            image = scale * back(masked) + RIDGE * direction
            alpha = norm_now / (jnp.sum(direction * image, axis=1, keepdims=True) + TINY)
            alphas.append(alpha)
            residual = residual - alpha * image
            norm_next = jnp.sum(residual * residual, axis=1, keepdims=True)
            direction = residual + norm_next / (norm_now + TINY) * direction
            norm_now = norm_next
        else:
            squared = jnp.sum(jnp.where(earlier, image_t * image_t, 0.0), axis=0)
            squared = lax.psum(squared, AXES)
            ridge_part = RIDGE * jnp.sum(direction * direction, axis=1, keepdims=True)
            small = jnp.concatenate(alphas + [norm_now, ridge_part], axis=1).T
            small = lax.all_gather(small, AXES, axis=1, tiled=True)
            small = small.reshape(ITERS + 1, spans, n_targets)
            all_seen = (span_ids * (tok_dev * feat_count)).astype(jnp.float32)
            all_scale = (1.0 / jnp.maximum(all_seen, 1.0))[:, None]
            last = small[ITERS - 1] / (all_scale * squared + small[ITERS] + TINY)
            steps = [small[i] for i in range(ITERS - 1)] + [last]
    predicted = 0.0
    for size, value in zip(steps, kept):
        mine = jnp.sum(jnp.where(here, size[None], 0.0), axis=1)
        predicted = predicted + mine * value
    predictions = predicted.astype(jnp.bfloat16)
    error = targets.astype(jnp.float32) - predictions.astype(jnp.float32)
    surprise = jnp.mean(error * error, axis=1)
    return (predictions, surprise)


def solution(mesh):
    return jax.shard_map(
        body,
        mesh=mesh,
        in_specs=(P(AXES, None), P(AXES, None), P(AXES)),
        out_specs=(P(AXES, None), P(AXES)),
        check_vma=False,
    )
```

```python
import jax
import jax.numpy as jnp
from jax import lax
from jax.sharding import PartitionSpec as P

ITERS = 3
RIDGE = 0.1
TINY = 1e-06
AXES = ("tm", "feat")


def body(activations, targets, span_of):
    spans = lax.axis_size("tm")
    feat_count = lax.axis_size("feat")
    devices = spans * feat_count
    tok_dev, width = activations.shape
    n_targets = targets.shape[1]
    rows = spans * n_targets
    own = rows // devices
    place = lax.axis_index("tm") * feat_count + lax.axis_index("feat")

    span_ids = jnp.arange(spans, dtype=jnp.int32)
    earlier = (span_of[:, None] < span_ids[None, :])[:, :, None]
    here = (span_of[:, None] == span_ids[None, :])[:, :, None]

    def back(masked):
        part = lax.dot_general(
            masked.reshape(tok_dev, rows),
            activations,
            (((0,), (0,)), ((), ())),
            preferred_element_type=jnp.float32,
        )
        part = part.reshape(spans, feat_count * own, width)
        part = lax.psum_scatter(part, "feat", scatter_dimension=1, tiled=True)
        pieces = lax.all_to_all(
            part.astype(jnp.bfloat16), "tm", split_axis=0, concat_axis=0, tiled=True
        )
        return jnp.sum(pieces.astype(jnp.float32), axis=0)

    row_span = (place * own + jnp.arange(own, dtype=jnp.int32)) // n_targets
    seen = (row_span * (tok_dev * feat_count)).astype(jnp.float32)
    scale = (1.0 / jnp.maximum(seen, 1.0))[:, None]

    zero = jnp.zeros((), targets.dtype)
    rhs = scale * back(jnp.where(earlier, targets[:, None, :], zero))
    residual = rhs
    direction = rhs
    norm_now = jnp.sum(rhs * rhs, axis=1, keepdims=True)
    alphas = []
    kept = []
    for step in range(ITERS):
        sent = direction.astype(jnp.bfloat16)
        direction = sent.astype(jnp.float32)
        everywhere = lax.all_gather(sent, AXES, axis=0, tiled=True)
        image_t = lax.dot_general(
            activations,
            everywhere,
            (((1,), (1,)), ((), ())),
            preferred_element_type=jnp.float32,
        ).reshape(tok_dev, spans, n_targets)
        kept.append(jnp.sum(jnp.where(here, image_t, 0.0), axis=1))
        if step + 1 < ITERS:
            masked = jnp.where(earlier, image_t, 0.0).astype(jnp.bfloat16)
            image = scale * back(masked) + RIDGE * direction
            alpha = norm_now / (jnp.sum(direction * image, axis=1, keepdims=True) + TINY)
            alphas.append(alpha)
            residual = residual - alpha * image
            norm_next = jnp.sum(residual * residual, axis=1, keepdims=True)
            direction = residual + norm_next / (norm_now + TINY) * direction
            norm_now = norm_next
        else:
            squared = jnp.sum(jnp.where(earlier, image_t * image_t, 0.0), axis=0)
            squared = lax.psum(squared, AXES)
            ridge_part = RIDGE * jnp.sum(direction * direction, axis=1, keepdims=True)
            small = jnp.concatenate(alphas + [norm_now, ridge_part], axis=1).T
            small = lax.all_gather(small, AXES, axis=1, tiled=True)
            small = small.reshape(ITERS + 1, spans, n_targets)
            all_seen = (span_ids * (tok_dev * feat_count)).astype(jnp.float32)
            all_scale = (1.0 / jnp.maximum(all_seen, 1.0))[:, None]
            last = small[ITERS - 1] / (all_scale * squared + small[ITERS] + TINY)
            steps = [small[i] for i in range(ITERS - 1)] + [last]
    predicted = 0.0
    for size, value in zip(steps, kept):
        mine = jnp.sum(jnp.where(here, size[None], 0.0), axis=1)
        predicted = predicted + mine * value
    predictions = predicted.astype(jnp.bfloat16)
    error = targets.astype(jnp.float32) - predictions.astype(jnp.float32)
    surprise = jnp.mean(error * error, axis=1)
    return (predictions, surprise)


def solution(mesh):
    return jax.shard_map(
        body,
        mesh=mesh,
        in_specs=(P(AXES, None), P(AXES, None), P(AXES)),
        out_specs=(P(AXES, None), P(AXES)),
        check_vma=False,
    )
```
